32 devices in a mesh: dp: 8 (over y, x, core), tensor: 4 (over z).
Axes of the slice: x: 2, y: 2, z: 4, core: 2. Of those that a mesh axis runs over, the one named last changes fastest.
Arguments:
- tokens: bfloat16 [80, 197, 768], P('dp', None, 'tensor'), may hold values from -6 to 6
- cotangent: bfloat16 [80, 197, 768], P('dp', None, 'tensor'), may hold values from -6 to 6
- live_count: int32 [8], P('dp'), may hold values from 1 to 10, as said below
- ln_scale: bfloat16 [2, 2, 768], P(None, None, 'tensor'), may hold values from 0.099609375 to 1.8984375
- ln_shift: bfloat16 [2, 2, 768], P(None, None, 'tensor'), may hold values from -3 to 3
- w_qkv: bfloat16 [2, 3, 768, 768], P(None, None, None, 'tensor'), may hold values from -0.21875 to 0.21875
- b_qv: bfloat16 [2, 2, 768], P(None, None, 'tensor'), may hold values from -3 to 3
- w_out: bfloat16 [2, 768, 768], P(None, 'tensor'), may hold values from -1.25 to 1.25
- b_out: bfloat16 [2, 768], P(None, 'tensor'), may hold values from -3 to 3
- w_up: bfloat16 [2, 768, 3072], P(None, None, 'tensor'), may hold values from -0.21875 to 0.21875
- b_up: bfloat16 [2, 3072], P(None, 'tensor'), may hold values from -3 to 3
- w_down: bfloat16 [2, 3072, 768], P(None, 'tensor'), may hold values from -0.109375 to 0.109375
- b_down: bfloat16 [2, 768], P(None, 'tensor'), may hold values from -3 to 3
Outputs:
- activations: bfloat16 [80, 197, 768], P('dp', None, 'tensor')
- grad_input: float32 [80, 197, 768], P('dp', None, 'tensor')
- grad_ln_scale: float32 [2, 2, 768], P(None, None, 'tensor')
- grad_ln_shift: float32 [2, 2, 768], P(None, None, 'tensor')
- grad_w_qkv: float32 [2, 3, 768, 768], P(None, None, None, 'tensor')
- grad_b_qv: float32 [2, 2, 768], P(None, None, 'tensor')
- grad_w_out: float32 [2, 768, 768], P(None, 'tensor')
- grad_b_out: float32 [2, 768], P(None, 'tensor')
- grad_w_up: float32 [2, 768, 3072], P(None, None, 'tensor')
- grad_b_up: float32 [2, 3072], P(None, 'tensor')
- grad_w_down: float32 [2, 3072, 768], P(None, 'tensor')
- grad_b_down: float32 [2, 768], P(None, 'tensor')
The draws below stay inside these ranges and needn't reach their ends.
Inputs may be any that keep to these rules, and one draw needn't show every extreme that they name: Dp index i holds live_count[i] images in its first slots; its other slots of 10 are empty; some index is full and some holds one image.
All inputs are finite; a program needn't handle non-finite values.
Results may differ from the reference program's by a relative error of at most 0.023.
Values may be sent and summed in bfloat16 or wider, within the bound.
A program may use at most 192 MiB of HBM per device.

```python
import jax
import jax.numpy as jnp
from jax import lax

HEAD = 64
D = 768
FF = 3072
SEQ = 197
SLOTS = 10
LAYERS = 2
IMAGES = 80
N_DP = 8
N_TENSOR = 4


def draw_live_count(key, part):
    key = jax.random.fold_in(key, 7)
    first_key, second_key = jax.random.split(key)
    counts = jax.random.randint(first_key, (N_DP,), 1, SLOTS + 1)
    place = jax.random.randint(second_key, (), 0, N_DP)
    counts = counts.at[place].set(SLOTS)
    counts = counts.at[(place + 1) % N_DP].set(1)
    return counts.astype(jnp.int32)


def steps_of(key, dims, shards, low, largest):
    loudness, own = 1.0, jax.random.fold_in(key, 6)
    for dim, shards_of in shards:
        draws = jnp.exp(jax.random.uniform(jax.random.fold_in(own, dim), (shards_of,), jnp.float32, low / len(shards), largest / len(shards)))
        loudness = loudness * jnp.repeat(draws, dims[dim] // shards_of).reshape([-1 if axis == dim else 1 for axis in range(len(dims))])
    return loudness


def scatter_about(stream_key, shape, scale, most, cuts=(), held_as=jnp.bfloat16):
    values = jax.random.normal(stream_key, shape, jnp.float32) * scale
    if len(cuts) > 0:
        values = steps_of(stream_key, shape, cuts, -0.22, 0.18) * values
    return jnp.clip(values, min=-most, max=most).astype(held_as)


def setup_inputs(seed: int = 0) -> dict:
    key_of = jax.random.split(jax.random.key(seed), 14)
    return {
        "tokens": scatter_about(key_of[0], (IMAGES, SEQ, D), 1.0, 6.0, ((0, 8), (2, 4))),
        "cotangent": scatter_about(key_of[1], (IMAGES, SEQ, D), 1.0, 6.0, ((0, 8), (2, 4))),
        "live_count": draw_live_count(jax.random.fold_in(key_of[13], 71), 0),
        "ln_scale": jnp.clip(1.0 + 0.18 * jax.random.normal(key_of[3], (LAYERS, 2, D), jnp.float32), 0.099609375, 1.8984375).astype(jnp.bfloat16),
        "ln_shift": scatter_about(key_of[4], (LAYERS, 2, D), 0.3, 3.0, ((2, 4),)),
        "w_qkv": scatter_about(key_of[5], (LAYERS, 3, D, D), D ** -0.5, 0.21875, ((3, 4),)),
        "b_qv": scatter_about(key_of[6], (LAYERS, 2, D), 0.3, 3.0, ((2, 4),)),
        "w_out": scatter_about(key_of[7], (LAYERS, D, D), (D // 32) ** -0.5, 1.25, ((1, 4),)),
        "b_out": scatter_about(key_of[8], (LAYERS, D), 0.3, 3.0, ((1, 4),)),
        "w_up": scatter_about(key_of[9], (LAYERS, D, FF), D ** -0.5, 0.21875, ((2, 4),)),
        "b_up": scatter_about(key_of[10], (LAYERS, FF), 0.3, 3.0, ((1, 4),)),
        "w_down": scatter_about(key_of[11], (LAYERS, FF, D), FF ** -0.5, 0.109375, ((1, 4),)),
        "b_down": scatter_about(key_of[12], (LAYERS, D), 0.3, 3.0, ((1, 4),)),
    }


EPSILON = 1e-06
HIGH = lax.Precision.HIGHEST

@jax.custom_vjp
def low(v):
    return lax.optimization_barrier(v.astype(jnp.bfloat16)).astype(jnp.float32)

@jax.custom_vjp
def low_back(v):
    return v

def low_keep(v):
    return (low(v), None)

def low_pass(kept, grad):
    return (grad,)

def back_keep(v):
    return (v, None)

def back_low(kept, grad):
    return (low(grad),)
low.defvjp(low_keep, low_pass)
low_back.defvjp(back_keep, back_low)

def layer_norm(values, gain, shift):
    center = values - lax.optimization_barrier(jnp.mean(values, -1, keepdims=True))
    return center * lax.rsqrt(lax.optimization_barrier(jnp.mean(center * center, -1, keepdims=True)) + EPSILON) * gain + shift

def product(form, left, right):
    return jnp.einsum(form, left, right, precision=HIGH)

def block_rows(left, right):
    width = left.shape[-1] // N_TENSOR
    total = low(product('std,de->ste', left[..., :width], right[:width]))
    for block in range(1, N_TENSOR):
        total = total + low(product('std,de->ste', left[..., block * width:(block + 1) * width], right[block * width:(block + 1) * width]))
    return low_back(total)

def block_columns(normed, matrices):
    width = matrices[0].shape[-1] // N_TENSOR
    pieces = [[] for matrix in matrices]
    for block in range(N_TENSOR):
        copied = low_back(normed)
        for which in range(len(matrices)):
            pieces[which].append(product('std,de->ste', copied, matrices[which][:, block * width:(block + 1) * width]))
    return [jnp.concatenate(group, -1) for group in pieces]

def encoder_layer(state, weights, layer_id):
    ln_scale, ln_shift, w_qkv, b_qv, w_out, b_out, w_up, b_up, w_down, b_down = weights
    slot_count, length, feat_width = state.shape
    head_count = feat_width // HEAD
    normed = low(layer_norm(state, ln_scale[layer_id, 0], ln_shift[layer_id, 0]))
    query_raw, key_raw, value_raw = block_columns(normed, [w_qkv[layer_id, 0], w_qkv[layer_id, 1], w_qkv[layer_id, 2]])
    queries = low(low_back(query_raw) + b_qv[layer_id, 0])
    key_rows = low(low_back(key_raw))
    values = low(low_back(value_raw) + b_qv[layer_id, 1])
    queries = queries.reshape(slot_count, length, head_count, HEAD)
    key_rows = key_rows.reshape(slot_count, length, head_count, HEAD)
    values = values.reshape(slot_count, length, head_count, HEAD)
    scores = low_back(product('sqhe,skhe->shqk', queries, key_rows)) * HEAD ** (-0.5)
    attention = low(jax.nn.softmax(scores, axis=-1))
    mixture = product('shqk,skhe->sqhe', attention, values).reshape(slot_count, length, feat_width)
    mixture = low(low_back(mixture))
    middle = low(state + block_rows(mixture, w_out[layer_id]) + b_out[layer_id])
    normed_two = low(layer_norm(middle, ln_scale[layer_id, 1], ln_shift[layer_id, 1]))
    hidden_raw = block_columns(normed_two, [w_up[layer_id]])[0]
    hidden = low_back(hidden_raw) + b_up[layer_id]
    active = low(jax.nn.gelu(hidden, approximate=False))
    return low(middle + block_rows(active, w_down[layer_id]) + b_down[layer_id])

def encode(group, weights):
    for layer_id in range(LAYERS):
        group = encoder_layer(group, weights, layer_id)
    return group

def reference(tokens, cotangent, live_count, ln_scale, ln_shift, w_qkv, b_qv, w_out, b_out, w_up, b_up, w_down, b_down):
    weights = tuple((array.astype(jnp.float32) for array in (ln_scale, ln_shift, w_qkv, b_qv, w_out, b_out, w_up, b_up, w_down, b_down)))
    groups = tokens.astype(jnp.float32).reshape(N_DP, SLOTS, SEQ, D)
    live_mask = (jnp.arange(SLOTS, dtype=jnp.int32)[None, :] < live_count[:, None]).astype(jnp.float32)[:, :, None, None]

    def forward(groups, *weights):

        def one_group(group):
            return encode(group, weights)
        return lax.map(jax.checkpoint(one_group), groups)
    outputs, pullback = jax.vjp(forward, groups, *weights)
    upstream = cotangent.astype(jnp.float32).reshape(N_DP, SLOTS, SEQ, D) * live_mask
    gradients = pullback(upstream)
    activations = (outputs * live_mask).astype(jnp.bfloat16).reshape(IMAGES, SEQ, D)
    grad_input = gradients[0].reshape(IMAGES, SEQ, D)
    return (activations, grad_input, gradients[1], gradients[2], gradients[3], gradients[4], gradients[5], gradients[6], gradients[7], gradients[8], gradients[9], gradients[10])
```

```python
import functools

import jax
import jax.numpy as jnp
from jax import lax
from jax.experimental import pallas as pl
from jax.experimental.pallas import tpu as pltpu
from jax.sharding import PartitionSpec as P

HEAD = 64
LAYERS = 2
EPSILON = 1e-06
ALL = ("tensor", "dp")
F32 = jnp.float32
BF16 = jnp.bfloat16
NN = (((1,), (0,)), ((), ()))
NT = (((1,), (1,)), ((), ()))
TN = (((0,), (0,)), ((), ()))


def mul(left, right, form):
    return lax.dot_general(left, right, form, preferred_element_type=F32)


def softmax_columns(keys, queries, length):
    scores = mul(keys, queries, NT) * HEAD ** (-0.5)
    row = lax.broadcasted_iota(jnp.int32, scores.shape, 0)
    scores = jnp.where(row < length, scores, -jnp.inf)
    raised = jnp.exp(scores - jnp.max(scores, 0, keepdims=True))
    return raised * (1.0 / jnp.sum(raised, 0, keepdims=True))


def attention_forward_kernel(qkv_ref, out_ref, *, length):
    width = out_ref.shape[1]
    for head in range(width // HEAD):
        at = head * HEAD
        q = qkv_ref[:, at : at + HEAD]
        k = qkv_ref[:, width + at : width + at + HEAD]
        v = qkv_ref[:, 2 * width + at : 2 * width + at + HEAD]
        probs = softmax_columns(k, q, length)
        out_ref[:, at : at + HEAD] = mul(probs.astype(BF16), v, TN).astype(BF16)


def attention_backward_kernel(qkv_ref, grad_ref, out_ref, *, length):
    width = grad_ref.shape[1]
    for head in range(width // HEAD):
        at = head * HEAD
        q = qkv_ref[:, at : at + HEAD]
        k = qkv_ref[:, width + at : width + at + HEAD]
        v = qkv_ref[:, 2 * width + at : 2 * width + at + HEAD]
        dm = grad_ref[:, at : at + HEAD]
        probs = softmax_columns(k, q, length)
        dp = mul(v, dm, NT)
        delta = jnp.sum(dp * probs, 0, keepdims=True)
        ds = (probs * (dp - delta) * HEAD ** (-0.5)).astype(BF16)
        out_ref[:, at : at + HEAD] = mul(ds, k, TN).astype(BF16)
        out_ref[:, width + at : width + at + HEAD] = mul(ds, q, NN).astype(BF16)
        out_ref[:, 2 * width + at : 2 * width + at + HEAD] = mul(
            probs.astype(BF16), dm, NN
        ).astype(BF16)


def attention_call(kernel, out_width, seq, length, *arrays):
    rows = arrays[0].shape[0]
    heads = arrays[0].shape[1] // (3 * HEAD)
    return pl.pallas_call(
        functools.partial(kernel, length=length),
        grid=(rows // seq,),
        in_specs=[pl.BlockSpec((seq, a.shape[1]), lambda b: (b, 0)) for a in arrays],
        out_specs=pl.BlockSpec((seq, out_width), lambda b: (b, 0)),
        out_shape=jax.ShapeDtypeStruct((rows, out_width), BF16),
        compiler_params=pltpu.CompilerParams(vmem_limit_bytes=32 * 2**20),
        cost_estimate=pl.CostEstimate(
            flops=rows * heads * seq * HEAD * 2 * (2 if len(arrays) == 1 else 5),
            bytes_accessed=rows * 2 * (out_width + sum(a.shape[1] for a in arrays)),
            transcendentals=rows * heads * seq,
        ),
    )(*arrays)


def normalize(values, gain, shift):
    center = values.astype(F32)
    center = center - jnp.mean(center, -1, keepdims=True)
    factor = lax.rsqrt(jnp.mean(center * center, -1, keepdims=True) + EPSILON)
    return (center * factor * gain + shift).astype(BF16)


def normalize_backward(values, gain, grad):
    center = values.astype(F32)
    center = center - jnp.mean(center, -1, keepdims=True)
    factor = lax.rsqrt(jnp.mean(center * center, -1, keepdims=True) + EPSILON)
    unit = center * factor
    gained = grad * gain
    back = factor * (
        gained
        - jnp.mean(gained, -1, keepdims=True)
        - unit * jnp.mean(gained * unit, -1, keepdims=True)
    )
    return back, jnp.sum(grad * unit, 0), jnp.sum(grad, 0)


def own_slice(matrix, rank, parts):
    size = matrix.shape[-1] // parts
    piece = lax.dynamic_slice_in_dim(matrix, rank * size, size, matrix.ndim - 1)
    return jnp.swapaxes(piece, -1, -2)


def own_rows(matrix, rank, parts):
    size = matrix.shape[-2] // parts
    return lax.dynamic_slice_in_dim(matrix, rank * size, size, matrix.ndim - 2)


def gather_all(part):
    return lax.all_gather(part, ALL, axis=0, tiled=False)


def on_device(
    tokens,
    cotangent,
    live_count,
    ln_scale,
    ln_shift,
    w_qkv,
    b_qv,
    w_out,
    b_out,
    w_up,
    b_up,
    w_down,
    b_down,
):
    slot_count, length, feat_width = tokens.shape
    n_dp = lax.axis_size("dp")
    n_tensor = lax.axis_size("tensor")
    devices = n_dp * n_tensor
    dp_rank = lax.axis_index("dp")
    tensor_rank = lax.axis_index("tensor")
    width = feat_width * n_tensor
    ff_width = w_up.shape[-1]
    each = -(-slot_count // n_tensor)
    seq = -(-length // 16) * 16
    rows = each * seq
    live_mask = (jnp.arange(slot_count, dtype=jnp.int32) < live_count[0])[:, None, None]

    def to_images(array):
        array = jnp.pad(array, ((0, each * n_tensor - slot_count), (0, 0), (0, 0)))
        array = array.reshape(n_tensor, each, length, feat_width)
        array = lax.all_to_all(array, "tensor", 0, 0)
        array = array.transpose(1, 2, 0, 3).reshape(each, length, width)
        return jnp.pad(array, ((0, 0), (0, seq - length), (0, 0))).reshape(rows, width)

    def to_slots(array):
        array = array.astype(BF16).reshape(each, seq, n_tensor, feat_width)[:, :length]
        array = lax.all_to_all(array.transpose(2, 0, 1, 3), "tensor", 0, 0)
        return array.reshape(each * n_tensor, length, feat_width)[:slot_count]

    small = [ln_scale, ln_shift, b_qv, b_out, b_up, b_down]
    flat = jnp.concatenate([a.reshape(-1) for a in small])
    flat = lax.all_gather(flat, "tensor", axis=0, tiled=False).astype(F32)
    full, start = [], 0
    for a in small:
        piece = flat[:, start : start + a.size].reshape((n_tensor,) + a.shape)
        start += a.size
        full.append(jnp.moveaxis(piece, 0, -2).reshape(a.shape[:-1] + (n_tensor * a.shape[-1],)))
    scale_f, shift_f, bqv_f, bout_f, bup_f, bdown_f = full

    head_rows = feat_width // n_dp
    up_rows = ff_width // n_dp
    weights = []
    for layer in range(LAYERS):
        one = jnp.concatenate(
            [
                own_slice(w_qkv[layer], dp_rank, n_dp).reshape(3 * head_rows, width),
                own_rows(w_out[layer], dp_rank, n_dp),
            ]
        )
        two = jnp.concatenate(
            [own_slice(w_up[layer], dp_rank, n_dp), own_rows(w_down[layer], dp_rank, n_dp)]
        )
        one = gather_all(one)
        two = gather_all(two)
        qkv_t = (
            one[:, : 3 * head_rows]
            .reshape(devices, 3, head_rows, width)
            .transpose(1, 0, 2, 3)
            .reshape(3 * width, width)
        )
        weights.append(
            (
                qkv_t,
                one[:, 3 * head_rows :].reshape(width, width),
                two[:, :up_rows].reshape(devices * up_rows, width),
                two[:, up_rows:].reshape(devices * up_rows, width),
            )
        )

    state = to_images(tokens)
    grad = to_images(jnp.where(live_mask, cotangent, jnp.zeros_like(cotangent)))
    stored = []
    for layer in range(LAYERS):
        qkv_t, out_w, up_t, down_w = weights[layer]
        normed = normalize(state, scale_f[layer, 0], shift_f[layer, 0])
        bias = jnp.concatenate([bqv_f[layer, 0], jnp.zeros((width,), F32), bqv_f[layer, 1]])
        qkv = (mul(normed, qkv_t, NT) + bias).astype(BF16)
        mixed = attention_call(attention_forward_kernel, width, seq, length, qkv)
        middle = (state.astype(F32) + mul(mixed, out_w, NN) + bout_f[layer]).astype(BF16)
        normed_two = normalize(middle, scale_f[layer, 1], shift_f[layer, 1])
        hidden = mul(normed_two, up_t, NT) + bup_f[layer]
        below = 0.5 + 0.5 * lax.erf(hidden * 0.5**0.5)
        active = (hidden * below).astype(BF16)
        slope = (below + hidden * jnp.exp(-0.5 * hidden * hidden) * 0.3989422804014327).astype(BF16)
        stored.append((state, normed, qkv, mixed, middle, normed_two, active, slope))
        state = (middle.astype(F32) + mul(active, down_w, NN) + bdown_f[layer]).astype(BF16)
    returned = to_slots(state)
    activations = jnp.where(live_mask, returned, jnp.zeros_like(returned))

    def reduce_all(array):
        array = lax.psum_scatter(array, ALL, scatter_dimension=0, tiled=True)
        return lax.all_gather(array, "dp", axis=0, tiled=False).astype(F32)

    upstream = grad.astype(F32)
    small_grads = [None] * LAYERS
    g_qkv, g_out, g_up, g_down = ([None] * LAYERS for _ in range(4))
    for layer in reversed(range(LAYERS)):
        qkv_t, out_w, up_t, down_w = weights[layer]
        state, normed, qkv, mixed, middle, normed_two, active, slope = stored[layer]
        low = upstream.astype(BF16)
        grad_b_down = jnp.sum(upstream, 0)
        grad_down = mul(active, low, TN).astype(BF16)
        grad_hidden = mul(low, down_w, NT) * slope.astype(F32)
        grad_b_up = jnp.sum(grad_hidden, 0)
        hidden_low = grad_hidden.astype(BF16)
        grad_up = mul(hidden_low, normed_two, TN).astype(BF16)
        two = jnp.concatenate(
            [
                grad_up.reshape(devices, up_rows, width),
                grad_down.reshape(devices, up_rows, width),
            ],
            axis=1,
        )
        two = reduce_all(two.reshape(devices * 2 * up_rows, width))
        g_up[layer] = two[:, :up_rows].reshape(ff_width, width).T
        g_down[layer] = two[:, up_rows:].reshape(ff_width, width)
        back, scale_two, shift_two = normalize_backward(
            middle, scale_f[layer, 1], mul(hidden_low, up_t, NN)
        )
        grad_middle = upstream + back
        grad_b_out = jnp.sum(grad_middle, 0)
        middle_low = grad_middle.astype(BF16)
        grad_out = mul(mixed, middle_low, TN).astype(BF16)
        grad_mixed = mul(middle_low, out_w, NT).astype(BF16)
        grad_qkv = attention_call(
            attention_backward_kernel, 3 * width, seq, length, qkv, grad_mixed
        )
        sums = jnp.sum(grad_qkv.astype(F32), 0)
        grad_b_qv = jnp.stack([sums[:width], sums[2 * width :]])
        grad_qkv_t = mul(grad_qkv, normed, TN).astype(BF16)
        one = jnp.concatenate(
            [
                grad_qkv_t.reshape(3, devices, head_rows, width)
                .transpose(1, 0, 2, 3)
                .reshape(devices, 3 * head_rows, width),
                grad_out.reshape(devices, head_rows, width),
            ],
            axis=1,
        )
        one = reduce_all(one.reshape(devices * 4 * head_rows, width))
        g_qkv[layer] = (
            one[:, : 3 * head_rows]
            .reshape(n_dp, 3, head_rows, width)
            .transpose(1, 3, 0, 2)
            .reshape(3, width, feat_width)
        )
        g_out[layer] = one[:, 3 * head_rows :].reshape(feat_width, width)
        back, scale_one, shift_one = normalize_backward(
            state, scale_f[layer, 0], mul(grad_qkv, qkv_t, NN)
        )
        upstream = grad_middle + back
        small_grads[layer] = (
            jnp.stack([scale_one, scale_two]),
            jnp.stack([shift_one, shift_two]),
            grad_b_qv,
            grad_b_out,
            grad_b_up,
            grad_b_down,
        )
    grad_input = to_slots(upstream).astype(F32)

    members = [jnp.stack([entry[i] for entry in small_grads]) for i in range(6)]
    flat = jnp.concatenate([m.reshape(-1) for m in members])
    flat = lax.psum(flat, ALL)
    out, start = [], 0
    for m in members:
        piece = flat[start : start + m.size].reshape(m.shape)
        start += m.size
        size = m.shape[-1] // n_tensor
        out.append(lax.dynamic_slice_in_dim(piece, tensor_rank * size, size, m.ndim - 1))
    return (
        activations,
        grad_input,
        out[0],
        out[1],
        jnp.stack(g_qkv),
        out[2],
        jnp.stack(g_out),
        out[3],
        jnp.stack(g_up),
        out[4],
        jnp.stack(g_down),
        out[5],
    )


def solution(mesh):
    placed = (
        P("dp", None, "tensor"),
        P("dp", None, "tensor"),
        P("dp"),
        P(None, None, "tensor"),
        P(None, None, "tensor"),
        P(None, None, None, "tensor"),
        P(None, None, "tensor"),
        P(None, "tensor", None),
        P(None, "tensor"),
        P(None, None, "tensor"),
        P(None, "tensor"),
        P(None, "tensor", None),
        P(None, "tensor"),
    )
    return jax.shard_map(
        on_device,
        mesh=mesh,
        in_specs=placed,
        out_specs=(
            P("dp", None, "tensor"),
            P("dp", None, "tensor"),
            P(None, None, "tensor"),
            P(None, None, "tensor"),
            P(None, None, None, "tensor"),
            P(None, None, "tensor"),
            P(None, "tensor", None),
            P(None, "tensor"),
            P(None, None, "tensor"),
            P(None, "tensor"),
            P(None, "tensor", None),
            P(None, "tensor"),
        ),
        check_vma=False,
    )
```

```python
import functools

import jax
import jax.numpy as jnp
from jax import lax
from jax.experimental import pallas as pl
from jax.experimental.pallas import tpu as pltpu
from jax.sharding import PartitionSpec as P

HEAD = 64
LAYERS = 2
EPSILON = 1e-06
ALL = ("tensor", "dp")
F32 = jnp.float32
BF16 = jnp.bfloat16
NN = (((1,), (0,)), ((), ()))
NT = (((1,), (1,)), ((), ()))
TN = (((0,), (0,)), ((), ()))


def mul(left, right, form):
    return lax.dot_general(left, right, form, preferred_element_type=F32)


def softmax_columns(keys, queries, length):
    scores = mul(keys, queries, NT) * HEAD ** (-0.5)
    row = lax.broadcasted_iota(jnp.int32, scores.shape, 0)
    scores = jnp.where(row < length, scores, -jnp.inf)
    raised = jnp.exp(scores - jnp.max(scores, 0, keepdims=True))
    return raised * (1.0 / jnp.sum(raised, 0, keepdims=True))


def attention_forward_kernel(qkv_ref, out_ref, *, length):
    width = out_ref.shape[1]
    for head in range(width // HEAD):
        at = head * HEAD
        q = qkv_ref[:, at : at + HEAD]
        k = qkv_ref[:, width + at : width + at + HEAD]
        v = qkv_ref[:, 2 * width + at : 2 * width + at + HEAD]
        probs = softmax_columns(k, q, length)
        out_ref[:, at : at + HEAD] = mul(probs.astype(BF16), v, TN).astype(BF16)


def attention_backward_kernel(qkv_ref, grad_ref, out_ref, *, length):
    width = grad_ref.shape[1]
    for head in range(width // HEAD):
        at = head * HEAD
        q = qkv_ref[:, at : at + HEAD]
        k = qkv_ref[:, width + at : width + at + HEAD]
        v = qkv_ref[:, 2 * width + at : 2 * width + at + HEAD]
        dm = grad_ref[:, at : at + HEAD]
        probs = softmax_columns(k, q, length)
        dp = mul(v, dm, NT)
        delta = jnp.sum(dp * probs, 0, keepdims=True)
        ds = (probs * (dp - delta) * HEAD ** (-0.5)).astype(BF16)
        out_ref[:, at : at + HEAD] = mul(ds, k, TN).astype(BF16)
        out_ref[:, width + at : width + at + HEAD] = mul(ds, q, NN).astype(BF16)
        out_ref[:, 2 * width + at : 2 * width + at + HEAD] = mul(
            probs.astype(BF16), dm, NN
        ).astype(BF16)


def attention_call(kernel, out_width, seq, length, *arrays):
    rows = arrays[0].shape[0]
    heads = arrays[0].shape[1] // (3 * HEAD)
    return pl.pallas_call(
        functools.partial(kernel, length=length),
        grid=(rows // seq,),
        in_specs=[pl.BlockSpec((seq, a.shape[1]), lambda b: (b, 0)) for a in arrays],
        out_specs=pl.BlockSpec((seq, out_width), lambda b: (b, 0)),
        out_shape=jax.ShapeDtypeStruct((rows, out_width), BF16),
        compiler_params=pltpu.CompilerParams(vmem_limit_bytes=32 * 2**20),
        cost_estimate=pl.CostEstimate(
            flops=rows * heads * seq * HEAD * 2 * (2 if len(arrays) == 1 else 5),
            bytes_accessed=rows * 2 * (out_width + sum(a.shape[1] for a in arrays)),
            transcendentals=rows * heads * seq,
        ),
    )(*arrays)


def normalize(values, gain, shift):
    center = values.astype(F32)
    center = center - jnp.mean(center, -1, keepdims=True)
    factor = lax.rsqrt(jnp.mean(center * center, -1, keepdims=True) + EPSILON)
    return (center * factor * gain + shift).astype(BF16)


def normalize_backward(values, gain, grad):
    center = values.astype(F32)
    center = center - jnp.mean(center, -1, keepdims=True)
    factor = lax.rsqrt(jnp.mean(center * center, -1, keepdims=True) + EPSILON)
    unit = center * factor
    gained = grad * gain
    back = factor * (
        gained
        - jnp.mean(gained, -1, keepdims=True)
        - unit * jnp.mean(gained * unit, -1, keepdims=True)
    )
    return back, jnp.sum(grad * unit, 0), jnp.sum(grad, 0)


def own_slice(matrix, rank, parts):
    size = matrix.shape[-1] // parts
    piece = lax.dynamic_slice_in_dim(matrix, rank * size, size, matrix.ndim - 1)
    return jnp.swapaxes(piece, -1, -2)


def own_rows(matrix, rank, parts):
    size = matrix.shape[-2] // parts
    return lax.dynamic_slice_in_dim(matrix, rank * size, size, matrix.ndim - 2)


def on_device(
    tokens,
    cotangent,
    live_count,
    ln_scale,
    ln_shift,
    w_qkv,
    b_qv,
    w_out,
    b_out,
    w_up,
    b_up,
    w_down,
    b_down,
):
    slot_count, length, feat_width = tokens.shape
    n_dp = lax.axis_size("dp")
    n_tensor = lax.axis_size("tensor")
    devices = n_dp * n_tensor
    dp_rank = lax.axis_index("dp")
    width = feat_width * n_tensor
    ff_width = w_up.shape[-1]
    each = -(-slot_count // n_tensor)
    seq = -(-length // 16) * 16
    rows = each * seq
    live_mask = (jnp.arange(slot_count, dtype=jnp.int32) < live_count[0])[:, None, None]

    def to_images(array):
        array = jnp.pad(array, ((0, each * n_tensor - slot_count), (0, 0), (0, 0)))
        array = array.reshape(n_tensor, each, length, feat_width)
        array = lax.all_to_all(array, "tensor", 0, 0)
        array = array.transpose(1, 2, 0, 3).reshape(each, length, width)
        return jnp.pad(array, ((0, 0), (0, seq - length), (0, 0))).reshape(rows, width)

    def to_slots(array):
        array = array.astype(BF16).reshape(each, seq, n_tensor, feat_width)[:, :length]
        array = lax.all_to_all(array.transpose(2, 0, 1, 3), "tensor", 0, 0)
        return array.reshape(each * n_tensor, length, feat_width)[:slot_count]

    head_rows = feat_width // n_dp
    up_rows = ff_width // n_dp
    used_rows = 4 * head_rows + 2 * up_rows
    slab_rows = -(-(used_rows + 1) // 16) * 16

    small = [ln_scale, ln_shift, b_qv, b_out, b_up, b_down]
    flat = jnp.concatenate([a.reshape(-1) for a in small])
    share = flat.size // n_dp
    extra = lax.dynamic_slice_in_dim(flat, dp_rank * share, share, 0)
    weights = []
    for layer in range(LAYERS):
        slab = jnp.concatenate(
            [
                own_slice(w_qkv[layer], dp_rank, n_dp).reshape(3 * head_rows, width),
                own_rows(w_out[layer], dp_rank, n_dp),
                own_slice(w_up[layer], dp_rank, n_dp),
                own_rows(w_down[layer], dp_rank, n_dp),
            ]
        )
        if layer == 0:
            last = jnp.pad(extra, (0, width - share))[None]
            slab = jnp.concatenate([slab, last])
        else:
            slab, gathered = lax.optimization_barrier((slab, gathered))
        slab = jnp.pad(slab, ((0, slab_rows - slab.shape[0]), (0, 0)))
        gathered = lax.all_gather(slab, ALL, axis=0, tiled=False)
        if layer == 0:
            flat = gathered[:, used_rows, :share].reshape(n_tensor, n_dp * share).astype(F32)
        at = 4 * head_rows
        weights.append(
            (
                gathered[:, : 3 * head_rows]
                .reshape(devices, 3, head_rows, width)
                .transpose(1, 0, 2, 3)
                .reshape(3 * width, width),
                gathered[:, 3 * head_rows : at].reshape(width, width),
                gathered[:, at : at + up_rows].reshape(devices * up_rows, width),
                gathered[:, at + up_rows : used_rows].reshape(devices * up_rows, width),
            )
        )
    full, start = [], 0
    for a in small:
        piece = flat[:, start : start + a.size].reshape((n_tensor,) + a.shape)
        start += a.size
        full.append(jnp.moveaxis(piece, 0, -2).reshape(a.shape[:-1] + (n_tensor * a.shape[-1],)))
    scale_f, shift_f, bqv_f, bout_f, bup_f, bdown_f = full

    state = to_images(tokens)
    grad = to_images(jnp.where(live_mask, cotangent, jnp.zeros_like(cotangent)))
    stored = []
    for layer in range(LAYERS):
        qkv_t, out_w, up_t, down_w = weights[layer]
        normed = normalize(state, scale_f[layer, 0], shift_f[layer, 0])
        bias = jnp.concatenate([bqv_f[layer, 0], jnp.zeros((width,), F32), bqv_f[layer, 1]])
        qkv = (mul(normed, qkv_t, NT) + bias).astype(BF16)
        mixed = attention_call(attention_forward_kernel, width, seq, length, qkv)
        middle = (state.astype(F32) + mul(mixed, out_w, NN) + bout_f[layer]).astype(BF16)
        normed_two = normalize(middle, scale_f[layer, 1], shift_f[layer, 1])
        hidden = mul(normed_two, up_t, NT) + bup_f[layer]
        below = 0.5 + 0.5 * lax.erf(hidden * 0.5**0.5)
        active = (hidden * below).astype(BF16)
        slope = (below + hidden * jnp.exp(-0.5 * hidden * hidden) * 0.3989422804014327).astype(BF16)
        stored.append((state, normed, qkv, mixed, middle, normed_two, active, slope))
        state = (middle.astype(F32) + mul(active, down_w, NN) + bdown_f[layer]).astype(BF16)
    returned = to_slots(state)
    activations = jnp.where(live_mask, returned, jnp.zeros_like(returned))

    upstream = grad.astype(F32)
    summed = [None] * LAYERS
    for layer in reversed(range(LAYERS)):
        qkv_t, out_w, up_t, down_w = weights[layer]
        state, normed, qkv, mixed, middle, normed_two, active, slope = stored[layer]
        low = upstream.astype(BF16)
        grad_b_down = jnp.sum(upstream, 0)
        grad_down = mul(active, low, TN).astype(BF16)
        grad_hidden = mul(low, down_w, NT) * slope.astype(F32)
        grad_b_up = jnp.sum(grad_hidden, 0)
        hidden_low = grad_hidden.astype(BF16)
        grad_up = mul(hidden_low, normed_two, TN).astype(BF16)
        back, scale_two, shift_two = normalize_backward(
            middle, scale_f[layer, 1], mul(hidden_low, up_t, NN)
        )
        grad_middle = upstream + back
        grad_b_out = jnp.sum(grad_middle, 0)
        middle_low = grad_middle.astype(BF16)
        grad_out = mul(mixed, middle_low, TN).astype(BF16)
        grad_mixed = mul(middle_low, out_w, NT).astype(BF16)
        grad_qkv = attention_call(
            attention_backward_kernel, 3 * width, seq, length, qkv, grad_mixed
        )
        sums = jnp.sum(grad_qkv.astype(F32), 0)
        grad_b_qv = jnp.stack([sums[:width], sums[2 * width :]])
        grad_qkv_t = mul(grad_qkv, normed, TN).astype(BF16)
        back, scale_one, shift_one = normalize_backward(
            state, scale_f[layer, 0], mul(grad_qkv, qkv_t, NN)
        )
        upstream = grad_middle + back
        members = [
            jnp.stack([scale_one, scale_two]),
            jnp.stack([shift_one, shift_two]),
            grad_b_qv,
            grad_b_out,
            grad_b_up,
            grad_b_down,
        ]
        flat = jnp.concatenate(
            [
                jnp.moveaxis(m.reshape(m.shape[:-1] + (n_tensor, -1)), -2, 0).reshape(n_tensor, -1)
                for m in members
            ],
            axis=1,
        )
        flat = flat.astype(BF16).reshape(devices, 1, -1)
        part = flat.shape[-1]
        slab = jnp.concatenate(
            [
                grad_qkv_t.reshape(3, devices, head_rows, width)
                .transpose(1, 0, 2, 3)
                .reshape(devices, 3 * head_rows, width),
                grad_out.reshape(devices, head_rows, width),
                grad_up.reshape(devices, up_rows, width),
                grad_down.reshape(devices, up_rows, width),
                jnp.pad(
                    flat, ((0, 0), (0, slab_rows - used_rows - 1), (0, width - part))
                ),
            ],
            axis=1,
        )
        if layer < LAYERS - 1:
            slab, summed[layer + 1] = lax.optimization_barrier((slab, summed[layer + 1]))
        summed[layer] = lax.psum_scatter(
            slab.reshape(devices * slab_rows, width), ALL, scatter_dimension=0, tiled=True
        )
    grad_input = to_slots(upstream).astype(F32)

    total = lax.all_gather(jnp.stack(summed), "dp", axis=0, tiled=False)
    at = 4 * head_rows
    g_qkv = (
        total[:, :, : 3 * head_rows]
        .reshape(n_dp, LAYERS, 3, head_rows, width)
        .transpose(1, 2, 4, 0, 3)
        .reshape(LAYERS, 3, width, feat_width)
        .astype(F32)
    )

    def by_rows(piece):
        return jnp.swapaxes(piece, 0, 1).reshape(LAYERS, -1, width).astype(F32)

    g_out = by_rows(total[:, :, 3 * head_rows : at])
    g_up = jnp.swapaxes(by_rows(total[:, :, at : at + up_rows]), 1, 2)
    g_down = by_rows(total[:, :, at + up_rows : used_rows])
    flat = jnp.swapaxes(total[:, :, used_rows, :part], 0, 1).reshape(LAYERS, -1).astype(F32)
    out, start = [], 0
    for m in members:
        size = m.size // n_tensor
        out.append(
            flat[:, start : start + size].reshape((LAYERS,) + m.shape[:-1] + (m.shape[-1] // n_tensor,))
        )
        start += size
    return (
        activations,
        grad_input,
        out[0],
        out[1],
        g_qkv,
        out[2],
        g_out,
        out[3],
        g_up,
        out[4],
        g_down,
        out[5],
    )


def solution(mesh):
    placed = (
        P("dp", None, "tensor"),
        P("dp", None, "tensor"),
        P("dp"),
        P(None, None, "tensor"),
        P(None, None, "tensor"),
        P(None, None, None, "tensor"),
        P(None, None, "tensor"),
        P(None, "tensor", None),
        P(None, "tensor"),
        P(None, None, "tensor"),
        P(None, "tensor"),
        P(None, "tensor", None),
        P(None, "tensor"),
    )
    return jax.shard_map(
        on_device,
        mesh=mesh,
        in_specs=placed,
        out_specs=(
            P("dp", None, "tensor"),
            P("dp", None, "tensor"),
            P(None, None, "tensor"),
            P(None, None, "tensor"),
            P(None, None, None, "tensor"),
            P(None, None, "tensor"),
            P(None, "tensor", None),
            P(None, "tensor"),
            P(None, None, "tensor"),
            P(None, "tensor"),
            P(None, "tensor", None),
            P(None, "tensor"),
        ),
        check_vma=False,
    )
```
